32 devices in a mesh: dp: 8 (over z, core), mp: 4 (over y, x).
Axes of the slice: x: 2, y: 2, z: 4, core: 2. Of those that a mesh axis runs over, the one named last changes fastest.
Arguments:
- tokens: bfloat16 [6144, 2048], P('dp'), may hold values from -20 to 20
- cotangent: bfloat16 [6144, 2048], P('dp'), may hold values from -6 to 6
- w_gate: bfloat16 [2048, 8192], P(None, 'mp'), may hold values from -1 to 1
- w_up: bfloat16 [2048, 8192], P(None, 'mp'), may hold values from -1 to 1
- w_down: bfloat16 [8192, 2048], P('mp'), may hold values from -0.0625 to 0.0625
- row_gate: float32 [2048], P('dp'), may hold values from 0.0003 to 20
- col_gate: float32 [8192], P('mp'), may hold values from 0.0003 to 10
- row_up: float32 [2048], P('dp'), may hold values from 0.0003 to 20
- col_up: float32 [8192], P('mp'), may hold values from 0.0003 to 10
- row_down: float32 [8192], P(('mp', 'dp')), may hold values from 0.01 to 300
- col_down: float32 [2048], replicated, may hold values from 0.01 to 300
Outputs:
- token_grad: bfloat16 [6144, 2048], P('dp', 'mp')
- update_gate: float32 [2048, 8192], P('dp', 'mp')
- update_up: float32 [2048, 8192], P('dp', 'mp')
- update_down: float32 [8192, 2048], P(('mp', 'dp'))
- row_gate_new: float32 [2048], P('dp')
- col_gate_new: float32 [8192], P('mp')
- row_up_new: float32 [2048], P('dp')
- col_up_new: float32 [8192], P('mp')
- row_down_new: float32 [8192], P(('mp', 'dp'))
- col_down_new: float32 [2048], replicated
The draws below stay inside these ranges and needn't reach their ends.
All inputs are finite; a program needn't handle non-finite values.
Results may differ from the reference program's by a relative error of at most 0.015.
Values may be sent and summed in bfloat16 or wider, within the bound.
A program may use at most 128 MiB of HBM per device.

```python
import jax
import jax.numpy as jnp
from jax import lax

D = 2048
FF = 8192
TOK_DEV = 768
TOKENS = 6144
N_DP = 8
N_MP = 4


def half_pattern(row_count, col_count, match_value, other_value):
    row_first = jnp.arange(row_count) < row_count // 2
    col_first = jnp.arange(col_count) < col_count // 2
    return jnp.where(row_first[:, None] == col_first[None, :], match_value, other_value).astype(jnp.float32)


def split_levels(key, length_all, first_low, first_high, second_low, second_high):
    fraction = jax.random.uniform(key, (length_all,), jnp.float32)
    first_half = jnp.arange(length_all) < length_all // 2
    low_end = jnp.log(jnp.where(first_half, first_low, second_low))
    high_end = jnp.log(jnp.where(first_half, first_high, second_high))
    return jnp.exp(low_end + fraction * (high_end - low_end)).astype(jnp.float32)


def draw_tokens(key, part):
    key = jax.random.fold_in(key, 11)
    base_key, jitter_key = jax.random.split(key)
    half_position = (jnp.arange(D) % (D // 2)).astype(jnp.float32) / (D // 2)
    base_values = jax.random.truncated_normal(base_key, -4.0, 4.0, (TOKENS, D), jnp.float32)
    spread = jnp.log(10.0)
    jitter = jax.random.uniform(jitter_key, (D,), jnp.float32, -0.35, 0.35)
    column_scale = jnp.exp(spread * (half_position - 1.0) + jitter)
    emphasis = half_pattern(TOKENS, D, 3.0, 1.0 / 3.0)
    return (base_values * column_scale[None, :] * emphasis).astype(jnp.bfloat16)


def draw_cotangent(key, part):
    key = jax.random.fold_in(key, 12)
    base_values = jax.random.truncated_normal(key, -4.0, 4.0, (TOKENS, D), jnp.float32)
    emphasis = half_pattern(TOKENS, D, 1.5, 0.5 / 3.0)
    return (base_values * emphasis).astype(jnp.bfloat16)


def draw_w_gate(key, part):
    key = jax.random.fold_in(key, 13)
    base_values = jax.random.truncated_normal(key, -4.0, 4.0, (D, FF), jnp.float32)
    levels = half_pattern(D, FF, 2.0, 0.5)
    return (base_values * levels * float(D) ** (-0.5)).astype(jnp.bfloat16)


def draw_w_up(key, part):
    key = jax.random.fold_in(key, 14)
    base_values = jax.random.truncated_normal(key, -4.0, 4.0, (D, FF), jnp.float32)
    levels = half_pattern(D, FF, 2.0, 0.5)
    return (base_values * levels * float(D) ** (-0.5)).astype(jnp.bfloat16)


def draw_row_gate(key, part):
    key = jax.random.fold_in(key, 21)
    return split_levels(key, D, 1.0, 2.0, 0.0003, 0.001)


def draw_col_gate(key, part):
    key = jax.random.fold_in(key, 22)
    return split_levels(key, FF, 0.0003, 0.001, 1.0, 2.0)


def draw_row_up(key, part):
    key = jax.random.fold_in(key, 23)
    return split_levels(key, D, 1.0, 2.0, 0.0003, 0.001)


def draw_col_up(key, part):
    key = jax.random.fold_in(key, 24)
    return split_levels(key, FF, 0.0003, 0.001, 1.0, 2.0)


def draw_row_down(key, part):
    key = jax.random.fold_in(key, 25)
    return split_levels(key, FF, 30.0, 60.0, 0.01, 0.03)


def draw_col_down(key, part):
    key = jax.random.fold_in(key, 26)
    return split_levels(key, D, 0.01, 0.03, 30.0, 60.0)


def block_scale(stream_key, shape, cuts, low, largest):
    factor_of, own = 1.0, jax.random.fold_in(stream_key, 6)
    for dim, blocks in cuts:
        steps = jnp.exp(jax.random.uniform(jax.random.fold_in(own, dim), (blocks,), jnp.float32, low / len(cuts), largest / len(cuts)))
        factor_of = factor_of * jnp.repeat(steps, shape[dim] // blocks).reshape([-1 if axis == dim else 1 for axis in range(len(shape))])
    return factor_of


def bell_draw(stream_key, dims, deviation, reach, pieces=(), dtype=jnp.bfloat16):
    array = jax.random.normal(stream_key, dims, jnp.float32) * deviation
    if len(pieces) > 0:
        array = block_scale(stream_key, dims, pieces, -0.22, 0.18) * array
    return jnp.clip(array, min=-reach, max=reach).astype(dtype)


def setup_inputs(seed: int = 0) -> dict:
    seeds = jax.random.split(jax.random.key(seed), 12)
    tokens = draw_tokens(jax.random.fold_in(seeds[11], 71), 0)
    cotangent = draw_cotangent(jax.random.fold_in(seeds[11], 71), 0)
    w_gate = draw_w_gate(jax.random.fold_in(seeds[11], 71), 0)
    w_up = draw_w_up(jax.random.fold_in(seeds[11], 71), 0)
    w_down = bell_draw(seeds[4], (FF, D), FF ** -0.5, 0.0625, ((0, 4),))
    row_gate = draw_row_gate(jax.random.fold_in(seeds[11], 71), 0)
    col_gate = draw_col_gate(jax.random.fold_in(seeds[11], 71), 0)
    row_up = draw_row_up(jax.random.fold_in(seeds[11], 71), 0)
    col_up = draw_col_up(jax.random.fold_in(seeds[11], 71), 0)
    row_down = draw_row_down(jax.random.fold_in(seeds[11], 71), 0)
    col_down = draw_col_down(jax.random.fold_in(seeds[11], 71), 0)
    return dict(tokens=tokens, cotangent=cotangent, w_gate=w_gate, w_up=w_up, w_down=w_down, row_gate=row_gate, col_gate=col_gate, row_up=row_up, col_up=col_up, row_down=row_down, col_down=col_down)


epsilon_one = 1e-30
decay_rate = 0.8

def silu_parts(gate_pre):
    sig = jax.nn.sigmoid(gate_pre)
    return (gate_pre * sig, sig * (1.0 + gate_pre * (1.0 - sig)))

def factored(grad, row_old, col_old):
    squares = grad * grad
    row_new = decay_rate * row_old + (1.0 - decay_rate) * (lax.optimization_barrier(jnp.mean(squares, 1)) + epsilon_one)
    col_new = decay_rate * col_old + (1.0 - decay_rate) * (lax.optimization_barrier(jnp.mean(squares, 0)) + epsilon_one)
    second = row_new[:, None] * col_new[None, :] / jnp.mean(row_new)
    raw = grad / jnp.sqrt(second)
    rms_value = jnp.sqrt(jnp.mean(raw * raw))
    return (raw / jnp.maximum(1.0, rms_value), row_new, col_new)

def reference(tokens, cotangent, w_gate, w_up, w_down, row_gate, col_gate, row_up, col_up, row_down, col_down):
    gate_pre = jnp.dot(tokens, w_gate, preferred_element_type=jnp.float32)
    up_pre = jnp.dot(tokens, w_up, preferred_element_type=jnp.float32)
    activated, derivative = silu_parts(gate_pre)
    hidden = (activated * up_pre).astype(jnp.bfloat16)
    hidden_grad = jnp.dot(cotangent, w_down.T, preferred_element_type=jnp.float32)
    grad_gate = (hidden_grad * up_pre * derivative).astype(jnp.bfloat16)
    grad_up = (hidden_grad * activated).astype(jnp.bfloat16)
    block_units = FF // N_MP
    token_total = jnp.zeros((TOKENS, D), jnp.float32)
    for block in range(N_MP):
        lower = block * block_units
        upper = lower + block_units
        partial_sum = jnp.dot(grad_gate[:, lower:upper], w_gate[:, lower:upper].T, preferred_element_type=jnp.float32)
        partial_sum = partial_sum + jnp.dot(grad_up[:, lower:upper], w_up[:, lower:upper].T, preferred_element_type=jnp.float32)
        rounded = lax.optimization_barrier(partial_sum.astype(jnp.bfloat16))
        token_total = token_total + rounded.astype(jnp.float32)
    token_grad = token_total.astype(jnp.bfloat16)
    grad_scale = float(TOKENS) ** (-0.5)
    g_gate = jnp.zeros((D, FF), jnp.float32)
    g_up = jnp.zeros((D, FF), jnp.float32)
    g_down = jnp.zeros((FF, D), jnp.float32)
    for block in range(N_DP):
        lower = block * TOK_DEV
        upper = lower + TOK_DEV
        term_gate = jnp.dot(tokens[lower:upper].T, grad_gate[lower:upper], preferred_element_type=jnp.float32) * grad_scale
        term_up = jnp.dot(tokens[lower:upper].T, grad_up[lower:upper], preferred_element_type=jnp.float32) * grad_scale
        term_down = jnp.dot(hidden[lower:upper].T, cotangent[lower:upper], preferred_element_type=jnp.float32) * grad_scale
        g_gate = g_gate + lax.optimization_barrier(term_gate.astype(jnp.bfloat16)).astype(jnp.float32)
        g_up = g_up + lax.optimization_barrier(term_up.astype(jnp.bfloat16)).astype(jnp.float32)
        g_down = g_down + lax.optimization_barrier(term_down.astype(jnp.bfloat16)).astype(jnp.float32)
    update_gate, row_gate_new, col_gate_new = factored(g_gate, row_gate, col_gate)
    update_up, row_up_new, col_up_new = factored(g_up, row_up, col_up)
    update_down, row_down_new, col_down_new = factored(g_down, row_down, col_down)
    return (token_grad, update_gate, update_up, update_down, row_gate_new, col_gate_new, row_up_new, col_up_new, row_down_new, col_down_new)
```

```python
import functools

import jax
import jax.numpy as jnp
from jax import lax
from jax.experimental import pallas as pl
from jax.experimental.pallas import tpu as pltpu
from jax.sharding import PartitionSpec as P

epsilon_one = 1e-30
decay_rate = 0.8
MESH = pl.DeviceIdType.MESH


def silu_parts(gate_pre):
    sig = jax.nn.sigmoid(gate_pre)
    return (gate_pre * sig, sig * (1.0 + gate_pre * (1.0 - sig)))


def moment_step(old_value, column_total, count):
    return decay_rate * old_value + (1.0 - decay_rate) * (column_total / count + epsilon_one)


def exchange_kernel(
    n_dp, n_mp, tail, dp_ref, mp_ref, dp_out, mp_out, dp_slots, mp_slots, d_send, d_recv, m_send, m_recv
):
    d = lax.axis_index("dp")
    m = lax.axis_index("mp")
    barrier = pltpu.get_barrier_semaphore()
    for k in range(1, n_dp):
        pl.semaphore_signal(
            barrier, inc=1, device_id=(lax.rem(d + k, n_dp), m), device_id_type=MESH
        )
    for k in range(1, n_mp):
        pl.semaphore_signal(
            barrier, inc=1, device_id=(d, lax.rem(m + k, n_mp)), device_id_type=MESH
        )
    pl.semaphore_wait(barrier, n_dp + n_mp - 2)

    dp_slots[0] = dp_ref[...]
    copies = []
    for k in range(1, n_dp):
        copies.append(
            pltpu.make_async_remote_copy(
                src_ref=dp_ref,
                dst_ref=dp_slots.at[k],
                send_sem=d_send.at[k],
                recv_sem=d_recv.at[k],
                device_id=(lax.rem(d + k, n_dp), m),
                device_id_type=MESH,
            )
        )
        copies[-1].start()
    for copy in copies:
        copy.wait()
    total = dp_slots[d]
    for j in range(1, n_dp):
        total = total + dp_slots[lax.rem(d - j + n_dp, n_dp)]
    dp_out[...] = total

    own_rows = mp_ref.shape[0]
    mp_slots[0, :own_rows] = mp_ref[...]
    mp_slots[0, own_rows:] = total[tail:]
    copies = []
    for k in range(1, n_mp):
        copies.append(
            pltpu.make_async_remote_copy(
                src_ref=mp_slots.at[0],
                dst_ref=mp_slots.at[k],
                send_sem=m_send.at[k],
                recv_sem=m_recv.at[k],
                device_id=(d, lax.rem(m + k, n_mp)),
                device_id_type=MESH,
            )
        )
        copies[-1].start()
    for copy in copies:
        copy.wait()
    total = mp_slots[m]
    for j in range(1, n_mp):
        total = total + mp_slots[lax.rem(m - j + n_mp, n_mp)]
    mp_out[...] = total


def exchange(dp_part, mp_part, tail, collective_id):
    n_dp, n_mp = lax.axis_size("dp"), lax.axis_size("mp")
    mp_rows = mp_part.shape[0] + dp_part.shape[0] - tail
    vmem = pl.BlockSpec(memory_space=pltpu.VMEM)
    return pl.pallas_call(
        functools.partial(exchange_kernel, n_dp, n_mp, tail),
        out_shape=(
            jax.ShapeDtypeStruct(dp_part.shape, jnp.float32),
            jax.ShapeDtypeStruct((mp_rows, 128), jnp.float32),
        ),
        in_specs=[vmem, vmem],
        out_specs=(vmem, vmem),
        scratch_shapes=[
            pltpu.VMEM((n_dp,) + dp_part.shape, jnp.float32),
            pltpu.VMEM((n_mp, mp_rows, 128), jnp.float32),
            pltpu.SemaphoreType.DMA((n_dp,)),
            pltpu.SemaphoreType.DMA((n_dp,)),
            pltpu.SemaphoreType.DMA((n_mp,)),
            pltpu.SemaphoreType.DMA((n_mp,)),
        ],
        compiler_params=pltpu.CompilerParams(
            collective_id=collective_id, has_side_effects=True, vmem_limit_bytes=8 * 2**20
        ),
    )(dp_part, mp_part)


def pack(*parts):
    flat = jnp.concatenate([part.reshape(-1) for part in parts])
    pad = -flat.shape[0] % 1024
    return jnp.pad(flat, (0, pad)).reshape(-1, 128)


def chain_scatter(blocks):
    n_dp = lax.axis_size("dp")
    count = n_dp // 2
    p = lax.axis_index("dp") // 2

    def pick(index):
        return lax.dynamic_index_in_dim(blocks, jnp.clip(index, 0, count - 1), 0, keepdims=False)

    from_left = from_right = None
    for step in range(1, count):
        to_right, to_left = pick(count - step + p), pick(step - count + p)
        if step > 1:
            to_right, to_left = to_right + from_left, to_left + from_right
        right_pairs = [
            (2 * q + c, 2 * q + 2 + c) for q in range(step) for c in range(2)
        ]
        left_pairs = [
            (2 * q + c, 2 * q - 2 + c)
            for q in range(count - step, count)
            for c in range(2)
        ]
        from_left = lax.ppermute(to_right, "dp", right_pairs)
        from_right = lax.ppermute(to_left, "dp", left_pairs)
    own = pick(p).astype(jnp.float32)
    return own + from_left.astype(jnp.float32) + from_right.astype(jnp.float32)


def body(
    tokens, cotangent, w_gate, w_up, w_down, row_gate, col_gate, row_up, col_up, row_down, col_down
):
    data_count = lax.axis_size("dp")
    model_count = lax.axis_size("mp")
    tok_rows, width_model = tokens.shape
    units = w_gate.shape[1]
    all_units = units * model_count
    grad_scale = float(tok_rows * data_count) ** (-0.5)
    core = lax.axis_index("dp") % 2
    swap = [(i, i ^ 1) for i in range(data_count)]
    chain = data_count // 2

    def halves(left_side):
        shaped = left_side.reshape(tok_rows, chain, 2, -1)

        def half(which):
            part = lax.dynamic_index_in_dim(shaped, which, 2, keepdims=False)
            return part.reshape(tok_rows, -1)

        return half(1 - core), half(core)

    def weight_term(left_side, right_side):
        return (
            jnp.einsum("tr,tc->rc", left_side, right_side, preferred_element_type=jnp.float32)
            * grad_scale
        ).astype(jnp.bfloat16)

    def pair_sum(parts, right_side):
        other, own = parts
        theirs = weight_term(other, right_side)
        received = lax.ppermute(theirs, "dp", swap)
        mine = weight_term(own, right_side)
        total = mine + received
        return theirs, mine, total.reshape(chain, -1, total.shape[1])

    gate_pre = jnp.dot(tokens, w_gate, preferred_element_type=jnp.float32)
    up_pre = jnp.dot(tokens, w_up, preferred_element_type=jnp.float32)
    activated, derivative = silu_parts(gate_pre)
    hidden = (activated * up_pre).astype(jnp.bfloat16)
    theirs, mine, blocks_down = pair_sum(halves(hidden), cotangent)
    cotangent_late, _, _ = lax.optimization_barrier((cotangent, theirs, mine))
    hidden_grad = jnp.einsum(
        "td,fd->tf", cotangent_late, w_down, preferred_element_type=jnp.float32
    )
    grad_gate = (hidden_grad * up_pre * derivative).astype(jnp.bfloat16)
    grad_up = (hidden_grad * activated).astype(jnp.bfloat16)
    token_halves = halves(tokens)
    theirs_g, mine_g, blocks_gate = pair_sum(token_halves, grad_gate)
    theirs_u, mine_u, blocks_up = pair_sum(token_halves, grad_up)
    grad_gate_late, grad_up_late, _, _, _, _ = lax.optimization_barrier(
        (grad_gate, grad_up, theirs_g, mine_g, theirs_u, mine_u)
    )
    input_terms = jnp.einsum("tf,df->td", grad_gate_late, w_gate, preferred_element_type=jnp.float32)
    input_terms = input_terms + jnp.einsum(
        "tf,df->td", grad_up_late, w_up, preferred_element_type=jnp.float32
    )
    token_grad = lax.psum_scatter(
        input_terms.astype(jnp.bfloat16), "mp", scatter_dimension=1, tiled=True
    )
    g_down = chain_scatter(blocks_down)
    g_gate = chain_scatter(blocks_gate)
    g_up = chain_scatter(blocks_up)

    squares_gate = g_gate * g_gate
    squares_up = g_up * g_up
    squares_down = g_down * g_down
    rows_gate, rows_up = jnp.sum(squares_gate, 1), jnp.sum(squares_up, 1)
    row_down_new = moment_step(row_down, jnp.sum(squares_down, 1), width_model)
    row_local = row_gate.shape[0]

    def new_row_share(row_old, row_part):
        old = decay_rate * jnp.sum(row_old) / model_count
        return old + (1.0 - decay_rate) * (
            jnp.sum(row_part) / all_units + row_local * epsilon_one / model_count
        )

    shares = jnp.stack(
        [new_row_share(row_gate, rows_gate), new_row_share(row_up, rows_up), jnp.sum(row_down_new)]
    )
    dp_part = pack(
        jnp.sum(squares_gate, 0), jnp.sum(squares_up, 0), jnp.sum(squares_down, 0), shares
    )
    mp_part = pack(rows_gate, rows_up)
    tail = 2 * units // 128
    dp_sum, mp_sum = exchange(dp_part, mp_part, tail, 0)
    col_sums = dp_sum[:tail].reshape(2, units)
    row_sums = mp_sum[: mp_part.shape[0]].reshape(-1)
    both = mp_sum[mp_part.shape[0] :].reshape(-1)
    row_counts = jnp.array([width_model, width_model, all_units], jnp.float32)
    row_means = both[width_model : width_model + 3] / row_counts
    row_gate_new = moment_step(row_gate, row_sums[:row_local], all_units)
    row_up_new = moment_step(row_up, row_sums[row_local : 2 * row_local], all_units)
    col_gate_new = moment_step(col_gate, col_sums[0], width_model)
    col_up_new = moment_step(col_up, col_sums[1], width_model)
    col_down_new = moment_step(col_down, both[:width_model], all_units)

    def raw_of(grad, row_new, col_new, row_mean):
        return grad * lax.rsqrt(row_new / row_mean)[:, None] * lax.rsqrt(col_new)[None, :]

    raw_gate = raw_of(g_gate, row_gate_new, col_gate_new, row_means[0])
    raw_up = raw_of(g_up, row_up_new, col_up_new, row_means[1])
    raw_down = raw_of(g_down, row_down_new, col_down_new, row_means[2])
    raw_parts = jnp.stack(
        [jnp.sum(raw_gate * raw_gate), jnp.sum(raw_up * raw_up), jnp.sum(raw_down * raw_down)]
    )
    _, raw_sum = exchange(pack(raw_parts), jnp.zeros((8, 128), jnp.float32), 0, 1)
    raw_totals = raw_sum[8, :3]
    divisor = jnp.maximum(1.0, jnp.sqrt(raw_totals / float(width_model * all_units)))
    update_gate = raw_gate / divisor[0]
    update_up = raw_up / divisor[1]
    update_down = raw_down / divisor[2]
    return (
        token_grad,
        update_gate,
        update_up,
        update_down,
        row_gate_new,
        col_gate_new,
        row_up_new,
        col_up_new,
        row_down_new,
        col_down_new,
    )


def solution(mesh):
    in_specs = (
        P("dp", None),
        P("dp", None),
        P(None, "mp"),
        P(None, "mp"),
        P("mp", None),
        P("dp"),
        P("mp"),
        P("dp"),
        P("mp"),
        P(("mp", "dp")),
        P(),
    )
    out_specs = (
        P("dp", "mp"),
        P("dp", "mp"),
        P("dp", "mp"),
        P(("mp", "dp"), None),
        P("dp"),
        P("mp"),
        P("dp"),
        P("mp"),
        P(("mp", "dp")),
        P(),
    )
    return jax.shard_map(body, mesh=mesh, in_specs=in_specs, out_specs=out_specs, check_vma=False)
```

```python
import functools

import jax
import jax.numpy as jnp
from jax import lax
from jax.experimental import pallas as pl
from jax.experimental.layout import Layout, with_layout_constraint
from jax.experimental.pallas import tpu as pltpu
from jax.sharding import PartitionSpec as P

epsilon_one = 1e-30
decay_rate = 0.8
MESH = pl.DeviceIdType.MESH


def silu_parts(gate_pre):
    sig = jax.nn.sigmoid(gate_pre)
    return (gate_pre * sig, sig * (1.0 + gate_pre * (1.0 - sig)))


def moment_step(old_value, column_total, count):
    return decay_rate * old_value + (1.0 - decay_rate) * (column_total / count + epsilon_one)


def exchange_kernel(
    n_dp, n_mp, tail, dp_ref, mp_ref, dp_out, mp_out, dp_slots, mp_slots, d_send, d_recv, m_send, m_recv
):
    d = lax.axis_index("dp")
    m = lax.axis_index("mp")
    barrier = pltpu.get_barrier_semaphore()
    for k in range(1, n_dp):
        pl.semaphore_signal(
            barrier, inc=1, device_id=(lax.rem(d + k, n_dp), m), device_id_type=MESH
        )
    for k in range(1, n_mp):
        pl.semaphore_signal(
            barrier, inc=1, device_id=(d, lax.rem(m + k, n_mp)), device_id_type=MESH
        )
    pl.semaphore_wait(barrier, n_dp + n_mp - 2)

    dp_slots[0] = dp_ref[...]
    copies = []
    for k in range(1, n_dp):
        copies.append(
            pltpu.make_async_remote_copy(
                src_ref=dp_ref,
                dst_ref=dp_slots.at[k],
                send_sem=d_send.at[k],
                recv_sem=d_recv.at[k],
                device_id=(lax.rem(d + k, n_dp), m),
                device_id_type=MESH,
            )
        )
        copies[-1].start()
    for copy in copies:
        copy.wait()
    total = dp_slots[d]
    for j in range(1, n_dp):
        total = total + dp_slots[lax.rem(d - j + n_dp, n_dp)]
    dp_out[...] = total

    own_rows = mp_ref.shape[0]
    mp_slots[0, :own_rows] = mp_ref[...]
    mp_slots[0, own_rows:] = total[tail:]
    copies = []
    for k in range(1, n_mp):
        copies.append(
            pltpu.make_async_remote_copy(
                src_ref=mp_slots.at[0],
                dst_ref=mp_slots.at[k],
                send_sem=m_send.at[k],
                recv_sem=m_recv.at[k],
                device_id=(d, lax.rem(m + k, n_mp)),
                device_id_type=MESH,
            )
        )
        copies[-1].start()
    for copy in copies:
        copy.wait()
    total = mp_slots[m]
    for j in range(1, n_mp):
        total = total + mp_slots[lax.rem(m - j + n_mp, n_mp)]
    mp_out[...] = total


def exchange(dp_part, mp_part, tail, collective_id):
    n_dp, n_mp = lax.axis_size("dp"), lax.axis_size("mp")
    mp_rows = mp_part.shape[0] + dp_part.shape[0] - tail
    vmem = pl.BlockSpec(memory_space=pltpu.VMEM)
    return pl.pallas_call(
        functools.partial(exchange_kernel, n_dp, n_mp, tail),
        out_shape=(
            jax.ShapeDtypeStruct(dp_part.shape, jnp.float32),
            jax.ShapeDtypeStruct((mp_rows, 128), jnp.float32),
        ),
        in_specs=[vmem, vmem],
        out_specs=(vmem, vmem),
        scratch_shapes=[
            pltpu.VMEM((n_dp,) + dp_part.shape, jnp.float32),
            pltpu.VMEM((n_mp, mp_rows, 128), jnp.float32),
            pltpu.SemaphoreType.DMA((n_dp,)),
            pltpu.SemaphoreType.DMA((n_dp,)),
            pltpu.SemaphoreType.DMA((n_mp,)),
            pltpu.SemaphoreType.DMA((n_mp,)),
        ],
        compiler_params=pltpu.CompilerParams(
            collective_id=collective_id, has_side_effects=True, vmem_limit_bytes=8 * 2**20
        ),
    )(dp_part, mp_part)


def pack(*parts):
    flat = jnp.concatenate([part.reshape(-1) for part in parts])
    pad = -flat.shape[0] % 1024
    return jnp.pad(flat, (0, pad)).reshape(-1, 128)


class Chain:
    def __init__(self, term):
        n_dp = lax.axis_size("dp")
        self.count = n_dp // 2
        self.core = lax.axis_index("dp") % 2
        self.place = lax.axis_index("dp") // 2
        self.term = term
        self.rows, width = term.shape[0] // n_dp, term.shape[1]
        paired = term.reshape(self.count, 2 * self.rows, width)
        theirs = lax.dynamic_slice_in_dim(paired, (1 - self.core) * self.rows, self.rows, 1)
        self.theirs = theirs.reshape(-1, width)
        self.received = lax.ppermute(self.theirs, "dp", [(i, i ^ 1) for i in range(n_dp)])
        self.from_left = self.from_right = None

    def pick(self, index):
        index = jnp.clip(index, 0, self.count - 1)
        own = lax.dynamic_slice_in_dim(self.term, (2 * index + self.core) * self.rows, self.rows)
        received = lax.dynamic_slice_in_dim(self.received, index * self.rows, self.rows)
        return own.astype(jnp.float32) + received.astype(jnp.float32)

    def advance(self, step, after):
        count, place = self.count, self.place
        to_right, to_left = self.pick(count - step + place), self.pick(step - count + place)
        if step > 1:
            to_right = to_right + self.from_left.astype(jnp.float32)
            to_left = to_left + self.from_right.astype(jnp.float32)
        payload = (to_right.astype(jnp.bfloat16), to_left.astype(jnp.bfloat16))
        to_right, to_left = lax.optimization_barrier(payload + after)[:2]
        right = [(2 * q + c, 2 * q + 2 + c) for q in range(step) for c in range(2)]
        left = [
            (2 * q + c, 2 * q - 2 + c) for q in range(count - step, count) for c in range(2)
        ]
        self.from_left, self.from_right = lax.optimization_barrier(
            (lax.ppermute(to_right, "dp", right), lax.ppermute(to_left, "dp", left))
        )
        return (to_right, to_left)

    def total(self):
        both = self.from_left.astype(jnp.float32) + self.from_right.astype(jnp.float32)
        return self.pick(self.place) + both


def body(
    tokens, cotangent, w_gate, w_up, w_down, row_gate, col_gate, row_up, col_up, row_down, col_down
):
    data_count = lax.axis_size("dp")
    model_count = lax.axis_size("mp")
    tok_rows, width_model = tokens.shape
    units = w_gate.shape[1]
    all_units = units * model_count
    grad_scale = float(tok_rows * data_count) ** (-0.5)
    chain = data_count // 2

    def weight_term(left_side, right_side):
        return (
            jnp.einsum("tr,tc->rc", left_side, right_side, preferred_element_type=jnp.float32)
            * grad_scale
        ).astype(jnp.bfloat16)

    def row_major(term):
        return with_layout_constraint(term, Layout(major_to_minor=(0, 1)))

    gate_pre = jnp.dot(tokens, w_gate, preferred_element_type=jnp.float32)
    up_pre = jnp.dot(tokens, w_up, preferred_element_type=jnp.float32)
    activated, derivative = silu_parts(gate_pre)
    hidden = (activated * up_pre).astype(jnp.bfloat16)
    down = Chain(row_major(weight_term(hidden, cotangent)))
    sent = down.advance(1, ())
    cotangent_late = lax.optimization_barrier((cotangent,) + sent)[0]
    hidden_grad = jnp.einsum(
        "td,fd->tf", cotangent_late, w_down, preferred_element_type=jnp.float32
    )
    grad_gate = (hidden_grad * up_pre * derivative).astype(jnp.bfloat16)
    grad_up = (hidden_grad * activated).astype(jnp.bfloat16)
    grad_gate_next = lax.optimization_barrier((grad_gate, down.from_left))[0]
    sent = down.advance(2, sent)
    gate = Chain(row_major(weight_term(tokens, grad_gate_next)))
    grad_up_next = lax.optimization_barrier((grad_up, gate.theirs, down.from_left))[0]
    up = Chain(row_major(weight_term(tokens, grad_up_next)))
    grad_gate_late, grad_up_late = grad_gate, grad_up
    order = []
    for step in range(1, chain):
        order += [(step + 0.0, down, step), (step + 1.5, gate, step), (step + 2.4, up, step)]
    for _, matrix, step in sorted(order, key=lambda entry: entry[0])[2:]:
        sent = matrix.advance(step, sent)
        if matrix is up and step == 1:
            grad_gate_late, grad_up_late = lax.optimization_barrier(
                (grad_gate, grad_up) + sent
            )[:2]
    input_terms = jnp.einsum("tf,df->td", grad_gate_late, w_gate, preferred_element_type=jnp.float32)
    input_terms = input_terms + jnp.einsum(
        "tf,df->td", grad_up_late, w_up, preferred_element_type=jnp.float32
    )
    token_grad = lax.psum_scatter(
        input_terms.astype(jnp.bfloat16), "mp", scatter_dimension=1, tiled=True
    )
    g_down = down.total()
    g_gate = gate.total()
    g_up = up.total()

    squares_gate = g_gate * g_gate
    squares_up = g_up * g_up
    squares_down = g_down * g_down
    rows_gate, rows_up = jnp.sum(squares_gate, 1), jnp.sum(squares_up, 1)
    row_down_new = moment_step(row_down, jnp.sum(squares_down, 1), width_model)
    row_local = row_gate.shape[0]

    def new_row_share(row_old, row_part):
        old = decay_rate * jnp.sum(row_old) / model_count
        return old + (1.0 - decay_rate) * (
            jnp.sum(row_part) / all_units + row_local * epsilon_one / model_count
        )

    shares = jnp.stack(
        [new_row_share(row_gate, rows_gate), new_row_share(row_up, rows_up), jnp.sum(row_down_new)]
    )
    dp_part = pack(
        jnp.sum(squares_gate, 0), jnp.sum(squares_up, 0), jnp.sum(squares_down, 0), shares
    )
    mp_part = pack(rows_gate, rows_up)
    tail = 2 * units // 128
    dp_sum, mp_sum = exchange(dp_part, mp_part, tail, 0)
    col_sums = dp_sum[:tail].reshape(2, units)
    row_sums = mp_sum[: mp_part.shape[0]].reshape(-1)
    both = mp_sum[mp_part.shape[0] :].reshape(-1)
    row_counts = jnp.array([width_model, width_model, all_units], jnp.float32)
    row_means = both[width_model : width_model + 3] / row_counts
    row_gate_new = moment_step(row_gate, row_sums[:row_local], all_units)
    row_up_new = moment_step(row_up, row_sums[row_local : 2 * row_local], all_units)
    col_gate_new = moment_step(col_gate, col_sums[0], width_model)
    col_up_new = moment_step(col_up, col_sums[1], width_model)
    col_down_new = moment_step(col_down, both[:width_model], all_units)

    def raw_of(grad, row_new, col_new, row_mean):
        return grad * lax.rsqrt(row_new / row_mean)[:, None] * lax.rsqrt(col_new)[None, :]

    raw_gate = raw_of(g_gate, row_gate_new, col_gate_new, row_means[0])
    raw_up = raw_of(g_up, row_up_new, col_up_new, row_means[1])
    raw_down = raw_of(g_down, row_down_new, col_down_new, row_means[2])
    raw_parts = jnp.stack(
        [jnp.sum(raw_gate * raw_gate), jnp.sum(raw_up * raw_up), jnp.sum(raw_down * raw_down)]
    )
    _, raw_sum = exchange(pack(raw_parts), jnp.zeros((8, 128), jnp.float32), 0, 1)
    raw_totals = raw_sum[8, :3]
    divisor = jnp.maximum(1.0, jnp.sqrt(raw_totals / float(width_model * all_units)))
    update_gate = raw_gate / divisor[0]
    update_up = raw_up / divisor[1]
    update_down = raw_down / divisor[2]
    return (
        token_grad,
        update_gate,
        update_up,
        update_down,
        row_gate_new,
        col_gate_new,
        row_up_new,
        col_up_new,
        row_down_new,
        col_down_new,
    )


def solution(mesh):
    in_specs = (
        P("dp", None),
        P("dp", None),
        P(None, "mp"),
        P(None, "mp"),
        P("mp", None),
        P("dp"),
        P("mp"),
        P("dp"),
        P("mp"),
        P(("mp", "dp")),
        P(),
    )
    out_specs = (
        P("dp", "mp"),
        P("dp", "mp"),
        P("dp", "mp"),
        P(("mp", "dp"), None),
        P("dp"),
        P("mp"),
        P("dp"),
        P("mp"),
        P(("mp", "dp")),
        P(),
    )
    return jax.shard_map(body, mesh=mesh, in_specs=in_specs, out_specs=out_specs, check_vma=False)
```
